512 devices in a mesh: dp: 64 (over y, z), group: 8 (over x, core).
Axes of the slice: x: 4, y: 4, z: 16, core: 2. Of those that a mesh axis runs over, the one named last changes fastest.
Arguments:
- queries: bfloat16 [32768, 3200], P(('group', 'dp')), parts along dimension 0, may hold values from -48 to 48
- latent: bfloat16 [32768, 320], P(('group', 'dp')), parts along dimension 0, may hold values from -4 to 4
- cache: bfloat16 [524288, 320], P(('group', 'dp')), parts along dimension 0, may hold values from -4 to 4
- residual: bfloat16 [32768, 1280], P(('group', 'dp')), parts along dimension 0, may hold values from -6 to 6
- value_up: bfloat16 [256, 1280], replicated, may hold values from -0.375 to 0.375
- norm_gain: float32 [1280], replicated, may hold values from 0.5 to 1.5
- cache_lengths: int32 [512], P(('group', 'dp')), parts along dimension 0, may hold values from 1 to 1024, as said below
- routes: int32 [32768, 6], P(('group', 'dp')), parts along dimension 0, may hold values from 0 to 31, all different within a row; in each aligned block of 64 rows (0 to 63, 64 to 127, ...) at most 18 rows name the same one
- route_gates: float32 [32768, 6], P(('group', 'dp')), parts along dimension 0, may hold values from 0.05 to 0.6
- expert_gate: bfloat16 [64, 1280, 384], P('dp'), may hold values from -0.15625 to 0.15625
- expert_up: bfloat16 [64, 1280, 384], P('dp'), may hold values from -0.15625 to 0.15625
- expert_down: bfloat16 [64, 384, 1280], P('dp'), may hold values from -0.21875 to 0.21875
Outputs:
- layer_out: bfloat16 [32768, 1280], P(('group', 'dp')), parts along dimension 0
The draws below stay inside these ranges and needn't reach their ends.
There are 8 independent parts, one for each index of `group`. The reference program is written for one: setup_inputs(seed, part) draws one part's arguments, and reference() takes and returns one part's arrays. A program takes and returns all parts, laid end to end along the dimension named above; an argument that names none is the same for every part. Nothing has to cross between parts.
Inputs may be any that keep to these rules, and one draw needn't show every extreme that they name: `routes`: in the rows of one rank no expert is chosen more than 18 times, and some expert is chosen exactly 18 times on some rank. `cache_lengths`: some rank has exactly 1024 earlier positions.
All inputs are finite; a program needn't handle non-finite values.
Results may differ from the reference program's by a relative error of at most 0.009.
Values may be sent and summed in bfloat16 or wider, within the bound.
No kernel may reach another device: no remote copies, remote signals or barrier semaphores. Data moves between devices by JAX's collectives and lax.ppermute only.
A program may use at most 64 MiB of HBM per device.

```python
import math
import jax
import jax.numpy as jnp
import numpy as np
from jax import lax

D = 1280
HEADS = 10
VHEAD = 128
LATENT = 256
ROPE = 64
MOE_FF = 768
TOP = 6
TOK_DEV = 64
PREFIX = 1024
EXPERTS = 32
CAP = 18
TOKENS = 4096
N_DP = 64


def latent_base(key):
    return jax.random.truncated_normal(key, -4.0, 4.0, (TOKENS, LATENT + ROPE), jnp.float32)


def draw_latent(key, part):
    base = latent_base(key)
    return base.astype(jnp.bfloat16)


def draw_cache(key, part):
    key = jax.random.fold_in(key, 31)
    values = jax.random.truncated_normal(key, -4.0, 4.0, (N_DP * PREFIX, LATENT + ROPE), jnp.float32)
    return values.astype(jnp.bfloat16)


def draw_cache_lengths(key, part):
    key = jax.random.fold_in(key, 41)
    first_key, second_key = jax.random.split(key)
    counts = jax.random.randint(first_key, (N_DP,), 1, PREFIX + 1, dtype=jnp.int32)
    fullest = jax.random.randint(second_key, (), 0, N_DP, dtype=jnp.int32)
    ranks = jnp.arange(N_DP, dtype=jnp.int32)
    return jnp.where(ranks == fullest, jnp.int32(PREFIX), counts)


def draw_queries(key, part):
    key = jax.random.fold_in(key, 23)
    width = LATENT + ROPE
    drawn = jax.random.truncated_normal(key, -4.0, 4.0, (TOKENS, HEADS * width), jnp.float32)
    return drawn.astype(jnp.bfloat16)


def shard_levels(rng, shape, pieces, smallest, high):
    loudness = 1.0
    for dim, shards_of in pieces:
        heights = jax.random.uniform(jax.random.fold_in(jax.random.fold_in(rng, 6), dim), (shards_of,), jnp.float32, smallest / len(pieces), high / len(pieces))
        loudness = loudness * jnp.repeat(jnp.exp(heights), shape[dim] // shards_of).reshape((-1,) + (1,) * (len(shape) - 1 - dim))
    return loudness


def shared_out(rng, own, number, rows, amount, top, bound, lean):
    order = jax.random.permutation(rng, amount)
    heavy_load, common = load_shares(amount, rows * top, bound, lean, True), load_shares(amount, rows * top, bound, lean, False)
    places = jnp.arange(amount)

    def named(tallies, turn):
        used = int((tallies > 0).sum())
        fixed = max(1, used // 4)
        shifted = fixed + (places - fixed + turn * (used - fixed)) % max(1, amount - fixed)
        return jnp.zeros((amount,), jnp.int32).at[order[jnp.where(places < fixed, places, shifted)]].set(jnp.asarray(tallies, jnp.int32))

    tallies = jnp.where(number % 4 == 0, named(heavy_load, number // 4), named(common, number - number // 4 - 1))
    mixed = jax.random.permutation(jax.random.fold_in(own, 3), amount)
    donor, receiver = mixed[0:amount // 2 * 2:2], mixed[1:amount // 2 * 2:2]
    room = jnp.minimum(tallies[donor] - 1, bound - tallies[receiver]) // 2
    room = jnp.where((donor == order[0]) | (receiver == order[0]) | (tallies[receiver] == 0), 0, jnp.maximum(room, 0))
    shifted = jax.random.randint(jax.random.fold_in(own, 4), (amount // 2,), 0, 1 << 20) % (room + 1)
    tallies = tallies.at[donor].add(-shifted).at[receiver].add(shifted)
    items = jnp.searchsorted(jnp.cumsum(tallies), jnp.arange(rows * top), side="right").astype(jnp.int32)
    grid = items.reshape(top, rows).T
    grid = grid[jax.random.permutation(jax.random.fold_in(own, 1), rows)]
    turn = jax.random.randint(jax.random.fold_in(own, 2), (rows, 1), 0, top)
    return jnp.take_along_axis(grid, (jnp.arange(top)[None, :] + turn) % top, axis=1)


def load_shares(number_of, total, reach, slope, full):
    loads = [(1 << 20) // math.isqrt(grade ** slope) + 1 for grade in range(1, number_of + 1)]
    largest = reach if full else min(reach, max(-(-total // number_of), total * loads[0] // sum(loads)))
    least = 1 if total - largest >= number_of - 1 else 0
    given, rest = [largest] + [least] * (number_of - 1), total - largest - least * (number_of - 1)
    while rest > 0:
        free = [i for i in range(1, number_of) if given[i] < largest] or [i for i in range(1, number_of) if given[i] < reach]
        whole, remaining = sum([loads[i] for i in free]), rest
        for i in free:
            addition = min(reach - given[i], max(1, remaining * loads[i] // whole), rest)
            given[i] = given[i] + addition
            rest = rest - addition
    return np.array(given)


def bell_draw(stream_key, extent, scale, reach, pieces=(), held_as=jnp.bfloat16):
    entries = scale * jax.random.normal(stream_key, extent, jnp.float32)
    if pieces:
        entries = entries * shard_levels(stream_key, extent, pieces, -0.22, 0.18)
    return jnp.clip(entries, -reach, reach).astype(held_as)


def setup_inputs(seed: int = 0, part: int = 0) -> dict:
    key_list = jax.random.split(jax.random.key(seed), 13)
    part_splits = jax.random.split(jax.random.fold_in(key_list[12], part), 13)
    queries = draw_queries(jax.random.fold_in(jax.random.fold_in(key_list[12], part), 71), part)
    latent = draw_latent(jax.random.fold_in(jax.random.fold_in(key_list[12], part), 71), part)
    cache = draw_cache(jax.random.fold_in(jax.random.fold_in(key_list[12], part), 71), part)
    residual = bell_draw(part_splits[3], (TOKENS, D), 1.0, 6.0, ((0, 64),))
    value_up = bell_draw(key_list[4], (LATENT, D), LATENT ** -0.5, 0.375)
    norm_gain = jnp.clip(1.0 + 0.1 * jax.random.normal(key_list[5], (D,), jnp.float32), 0.5, 1.5)
    cache_lengths = draw_cache_lengths(jax.random.fold_in(jax.random.fold_in(key_list[12], part), 71), part)
    routes_keys = jax.random.split(jax.random.fold_in(part_splits[7], 1), TOKENS // TOK_DEV)
    routes_turns = jax.random.permutation(jax.random.fold_in(part_splits[7], 3), TOKENS // TOK_DEV)
    routes = jax.vmap(lambda own, number: shared_out(jax.random.fold_in(part_splits[7], 2), own, number, TOK_DEV, EXPERTS, TOP, CAP, 2))(routes_keys, routes_turns).reshape((TOKENS, TOP))
    route_gates = jnp.clip(0.05 + 0.55 * jax.random.uniform(part_splits[8], (TOKENS, TOP), jnp.float32) ** shard_levels(part_splits[8], (TOKENS, TOP), ((0, 64),), -0.2, 0.2), 0.05, 0.6)
    expert_gate = bell_draw(key_list[9], (N_DP, D, MOE_FF // 2), D ** -0.5, 0.15625, ((0, 64),))
    expert_up = bell_draw(key_list[10], (N_DP, D, MOE_FF // 2), D ** -0.5, 0.15625, ((0, 64),))
    expert_down = bell_draw(key_list[11], (N_DP, MOE_FF // 2, D), MOE_FF ** -0.5, 0.21875, ((0, 64),))
    return dict(queries=queries, latent=latent, cache=cache, residual=residual, value_up=value_up, norm_gain=norm_gain, cache_lengths=cache_lengths, routes=routes, route_gates=route_gates, expert_gate=expert_gate, expert_up=expert_up, expert_down=expert_down)


def attend_rank(query_rows, latent_rows, cache_rows, residual_rows, cache_length, value_up):
    count_rows = query_rows.shape[0]
    stacked = query_rows.astype(jnp.float32).reshape(count_rows, HEADS, LATENT + ROPE)
    keys = jnp.concatenate([cache_rows, latent_rows], axis=0).astype(jnp.float32)
    scores = jnp.einsum('thd,sd->hts', stacked, keys) * (VHEAD + ROPE) ** (-0.5)
    positions = jnp.arange(count_rows, dtype=jnp.int32)
    key_index = jnp.arange(PREFIX + count_rows, dtype=jnp.int32)
    from_cache = key_index[None, :] < cache_length
    from_new = (key_index[None, :] >= PREFIX) & (key_index[None, :] - PREFIX <= positions[:, None])
    allowed = from_cache | from_new
    scores = jnp.where(allowed[None], scores, jnp.float32(-1e+30))
    largest = lax.optimization_barrier(jnp.max(scores, axis=2, keepdims=True))
    exponent = jnp.exp(scores - largest)
    attention = (exponent / lax.optimization_barrier(jnp.sum(exponent, axis=2, keepdims=True))).astype(jnp.bfloat16)
    mixed_latent = jnp.einsum('hts,sr->thr', attention.astype(jnp.float32), keys[:, :LATENT]).astype(jnp.bfloat16)
    values = jnp.einsum('thr,rhv->thv', mixed_latent.astype(jnp.float32), value_up.astype(jnp.float32).reshape(LATENT, HEADS, VHEAD)).reshape(count_rows, D)
    return (residual_rows.astype(jnp.float32) + values).astype(jnp.bfloat16)

def reference(queries, latent, cache, residual, value_up, norm_gain, cache_lengths, routes, route_gates, expert_gate, expert_up, expert_down):
    middle = lax.map(lambda items: attend_rank(items[0], items[1], items[2], items[3], items[4], value_up), (queries.reshape(N_DP, TOK_DEV, -1), latent.reshape(N_DP, TOK_DEV, -1), cache.reshape(N_DP, PREFIX, -1), residual.reshape(N_DP, TOK_DEV, -1), cache_lengths))
    middle = middle.reshape(TOKENS, D)
    middle_f = middle.astype(jnp.float32)
    normed = (middle_f * lax.rsqrt(lax.optimization_barrier(jnp.mean(middle_f * middle_f, axis=1, keepdims=True)) + 1e-06) * norm_gain).astype(jnp.bfloat16)

    def expert_step(total, expert):
        halves = []
        for half in range(2):
            index = 2 * expert + half
            gate = jnp.dot(normed, expert_gate[index], preferred_element_type=jnp.float32)
            upper = jnp.dot(normed, expert_up[index], preferred_element_type=jnp.float32)
            hidden = (jax.nn.silu(gate) * upper).astype(jnp.bfloat16)
            halves.append(jnp.dot(hidden, expert_down[index], preferred_element_type=jnp.float32).astype(jnp.bfloat16))
        expert_out = (halves[0].astype(jnp.float32) + halves[1].astype(jnp.float32)).astype(jnp.bfloat16)
        weight = lax.optimization_barrier(jnp.sum(jnp.where(routes == expert, route_gates, jnp.float32(0.0)), axis=1))
        return (total + weight[:, None] * expert_out.astype(jnp.float32), None)
    mixture, _ = lax.scan(expert_step, jnp.zeros((TOKENS, D), jnp.float32), jnp.arange(EXPERTS, dtype=jnp.int32))
    return (middle_f + mixture).astype(jnp.bfloat16)
```

```python
import jax
import jax.numpy as jnp
import numpy as np
from jax import lax
from jax.sharding import PartitionSpec as P

HEADS = 10
VHEAD = 128
LATENT = 256
ROPE = 64
TOP = 6
NY = 4
NZ = 16
CAP = 18
EXPERTS = 32
EXTRA = 128

FAR = [[y * NZ + 4 * q + r for q in range(4)] for y in range(NY) for r in range(4)]
NEAR = [
    [y * NZ + (2 * k + 1 + s) % NZ for y in range(NY) for s in range(2)] for k in range(NZ // 2)
]
SWAP = [(i, i ^ 1) for i in range(NY * NZ)]


def dot32(a, b):
    return jnp.dot(a, b, preferred_element_type=jnp.float32)


def other_half(weight):
    rows = weight.shape[0] // 8
    mine = lax.dynamic_slice_in_dim(weight, lax.axis_index("group") * rows, rows, axis=0)
    theirs = lax.ppermute(mine, "dp", SWAP)
    return lax.all_gather(theirs, "group", axis=0, tiled=True)


def attend(queries, latent, cache, residual, value_up, norm_gain, cache_lengths):
    rows_here = queries.shape[0]
    prefix_rows = cache.shape[0]
    stacked = queries.reshape(rows_here, HEADS, LATENT + ROPE)
    keys = jnp.concatenate([cache, latent], axis=0)
    scores = jnp.einsum("thd,sd->hts", stacked, keys, preferred_element_type=jnp.float32) * (
        VHEAD + ROPE
    ) ** (-0.5)
    positions = jnp.arange(rows_here, dtype=jnp.int32)
    key_index = jnp.arange(prefix_rows + rows_here, dtype=jnp.int32)
    from_cache = key_index[None, :] < cache_lengths[0]
    from_new = (key_index[None, :] >= prefix_rows) & (
        key_index[None, :] - prefix_rows <= positions[:, None]
    )
    allowed = from_cache | from_new
    scores = jnp.where(allowed[None], scores, jnp.float32(-1e30))
    largest = jnp.max(scores, axis=2, keepdims=True)
    exponent = jnp.exp(scores - largest)
    attention = (exponent / jnp.sum(exponent, axis=2, keepdims=True)).astype(jnp.bfloat16)
    mixed_latent = jnp.einsum(
        "hts,sr->thr", attention, keys[:, :LATENT], preferred_element_type=jnp.float32
    ).astype(jnp.bfloat16)
    values = jnp.einsum(
        "thr,rhv->thv",
        mixed_latent,
        value_up.reshape(LATENT, HEADS, VHEAD),
        preferred_element_type=jnp.float32,
    ).reshape(rows_here, HEADS * VHEAD)
    middle = (residual.astype(jnp.float32) + values).astype(jnp.bfloat16)
    middle_f = middle.astype(jnp.float32)
    normed = (
        middle_f
        * lax.rsqrt(jnp.mean(middle_f * middle_f, axis=1, keepdims=True) + 1e-06)
        * norm_gain
    ).astype(jnp.bfloat16)
    return middle, normed


def gate_columns(routes, route_gates):
    dense = jnp.sum(
        jnp.where(
            routes[:, :, None] == jnp.arange(EXPERTS, dtype=jnp.int32), route_gates[:, :, None], 0.0
        ),
        axis=1,
    )
    high = dense.astype(jnp.bfloat16)
    low = (dense - high.astype(jnp.float32)).astype(jnp.bfloat16)
    pad = jnp.zeros((routes.shape[0], EXTRA - 2 * EXPERTS), jnp.bfloat16)
    return jnp.concatenate([high, low, pad], axis=1)


def select_matrix(gates, near):
    cols = gates.astype(jnp.float32)
    dense = (cols[:, :, :EXPERTS] + cols[:, :, EXPERTS : 2 * EXPERTS]).reshape(-1, EXPERTS)
    member = jnp.arange(8, dtype=jnp.int32)
    expert = (member // 2) * 8 + (near + member % 2) % 8
    pick = (expert[:, None] == jnp.arange(EXPERTS, dtype=jnp.int32)[None, :]).astype(jnp.float32)
    chosen = jnp.einsum("ce,je->jc", dense, pick, precision=lax.Precision.HIGHEST)
    taken = chosen > 0
    ranks = chosen.shape[1] // 64
    counts = jnp.cumsum(taken.reshape(8, ranks, 64).astype(jnp.int32), axis=2) - 1
    slot = counts + CAP * jnp.arange(ranks, dtype=jnp.int32)[None, :, None]
    slot = jnp.where(taken, slot.reshape(8, -1), -1)
    sel = slot[:, None, :] == jnp.arange(CAP * ranks, dtype=jnp.int32)[None, :, None]
    return sel, chosen


def on_device(
    queries,
    latent,
    cache,
    residual,
    value_up,
    norm_gain,
    cache_lengths,
    routes,
    route_gates,
    expert_gate,
    expert_up,
    expert_down,
):
    gate_a, up_a, down_a = expert_gate[0], expert_up[0], expert_down[0]
    gate_b, up_b, down_b = other_half(gate_a), other_half(up_a), other_half(down_a)
    middle, normed = attend(queries, latent, cache, residual, value_up, norm_gain, cache_lengths)
    width = normed.shape[1]
    position = lax.axis_index("dp") % NZ
    near = ((position + NZ - 1) % NZ) // 2

    payload = jnp.concatenate([normed, gate_columns(routes, route_gates)], axis=1)
    spread = jnp.broadcast_to(payload[None], (4,) + payload.shape)
    hub = lax.all_to_all(
        spread, "dp", split_axis=0, concat_axis=0, axis_index_groups=FAR, tiled=True
    )
    sel, chosen = select_matrix(hub[:, :, width:], near)
    outgoing = jnp.einsum(
        "jic,cd->jid",
        sel.astype(jnp.bfloat16),
        hub[:, :, :width].reshape(-1, width),
        preferred_element_type=jnp.float32,
    ).astype(jnp.bfloat16)
    arrived = lax.all_to_all(
        outgoing, "dp", split_axis=0, concat_axis=0, axis_index_groups=NEAR, tiled=True
    ).reshape(-1, width)

    hidden_a = (jax.nn.silu(dot32(arrived, gate_a)) * dot32(arrived, up_a)).astype(jnp.bfloat16)
    hidden_b = (jax.nn.silu(dot32(arrived, gate_b)) * dot32(arrived, up_b)).astype(jnp.bfloat16)
    expert_out = (dot32(hidden_a, down_a) + dot32(hidden_b, down_b)).astype(jnp.bfloat16)
    returned = lax.all_to_all(
        expert_out.reshape(outgoing.shape),
        "dp",
        split_axis=0,
        concat_axis=0,
        axis_index_groups=NEAR,
        tiled=True,
    )
    weight = jnp.where(sel, chosen[:, None, :], 0.0)
    high = weight.astype(jnp.bfloat16)
    low = (weight - high.astype(jnp.float32)).astype(jnp.bfloat16)
    mixed = jnp.einsum("jic,jid->cd", high, returned, preferred_element_type=jnp.float32)
    mixed = mixed + jnp.einsum("jic,jid->cd", low, returned, preferred_element_type=jnp.float32)
    back = lax.all_to_all(
        mixed.astype(jnp.bfloat16).reshape(4, 64, width),
        "dp",
        split_axis=0,
        concat_axis=0,
        axis_index_groups=FAR,
        tiled=True,
    )
    mixture = jnp.sum(back.astype(jnp.float32), axis=0)
    return (middle.astype(jnp.float32) + mixture).astype(jnp.bfloat16)


def solution(mesh):
    return jax.shard_map(
        on_device,
        mesh=mesh,
        in_specs=(
            P(("group", "dp"), None),
            P(("group", "dp"), None),
            P(("group", "dp"), None),
            P(("group", "dp"), None),
            P(),
            P(),
            P(("group", "dp")),
            P(("group", "dp"), None),
            P(("group", "dp"), None),
            P("dp", None, None),
            P("dp", None, None),
            P("dp", None, None),
        ),
        out_specs=P(("group", "dp"), None),
        check_vma=False,
    )
```

```python
import jax
import jax.numpy as jnp
from jax import lax
from jax.experimental import pallas as pl
from jax.experimental.pallas import tpu as pltpu
from jax.sharding import PartitionSpec as P

HEADS = 10
VHEAD = 128
LATENT = 256
ROPE = 64
KEY = LATENT + ROPE
TOP = 6
NY = 4
NZ = 16
CAP = 18
EXPERTS = 32
EXTRA = 128
GROUP = 8
RANKS = 4
MEMBERS = 8
SLOTS = RANKS * CAP
TOK = 64
D = 1280
FF = 384

FAR = [[y * NZ + 4 * q + r for q in range(4)] for y in range(NY) for r in range(4)]
NEAR = [
    [y * NZ + (2 * k + 1 + s) % NZ for y in range(NY) for s in range(2)] for k in range(NZ // 2)
]
SWAP = [(i, i ^ 1) for i in range(NY * NZ)]

VMEM = pl.BlockSpec(memory_space=pltpu.VMEM)
SMEM = pl.BlockSpec(memory_space=pltpu.SMEM)
ANY = pl.BlockSpec(memory_space=pl.ANY)


def dot32(a, b):
    return jnp.dot(a, b, preferred_element_type=jnp.float32)


def dot_nt(a, b):
    return lax.dot_general(a, b, (((1,), (1,)), ((), ())), preferred_element_type=jnp.float32)


def iota(shape, dim):
    return lax.broadcasted_iota(jnp.int32, shape, dim)


GROWS = D // GROUP
DROWS = FF // GROUP
GBLOCKS = FF // 128
DBLOCKS = D // 128
PACKED = 2 * GBLOCKS * GROWS + DBLOCKS * DROWS


def pack_kernel(mine_ref, gate_ref, up_ref, down_ref, out_ref, sem):
    mine = mine_ref[0]
    copies = []
    at = 0
    for ref, rows, blocks in ((gate_ref, GROWS, GBLOCKS), (up_ref, GROWS, GBLOCKS), (down_ref, DROWS, DBLOCKS)):
        for c in range(blocks):
            copies.append(
                pltpu.make_async_copy(
                    ref.at[mine, :, pl.ds(c * 128, 128)], out_ref.at[pl.ds(at, rows), :], sem.at[len(copies)]
                )
            )
            at += rows
    for copy in copies:
        copy.start()
    for copy in copies:
        copy.wait()


def pack(mine, gate, up, down):
    return pl.pallas_call(
        pack_kernel,
        out_shape=jax.ShapeDtypeStruct((PACKED, 128), jnp.bfloat16),
        in_specs=[SMEM, ANY, ANY, ANY],
        out_specs=ANY,
        scratch_shapes=[pltpu.SemaphoreType.DMA((2 * GBLOCKS + DBLOCKS,))],
        cost_estimate=pl.CostEstimate(flops=0, bytes_accessed=2 * PACKED * 256, transcendentals=0),
        name="pack",
    )(mine, gate.reshape(GROUP, GROWS, FF), up.reshape(GROUP, GROWS, FF), down.reshape(GROUP, DROWS, D))


def attend_kernel(
    length_ref, q_ref, latent_ref, cache_ref, residual_ref, value_up_ref, gain_ref, routes_ref, gates_ref,
    payload_ref, middle_ref, q_s, mid_s,
):
    scale = (VHEAD + ROPE) ** (-0.5)
    for h in range(HEADS):
        q_s[h * TOK : (h + 1) * TOK, :] = q_ref[:, h * KEY : (h + 1) * KEY]
    length = length_ref[0]
    prefix = cache_ref.shape[0]
    bias = jnp.where(iota((1, prefix), 1) < length, 0.0, -1e30).astype(jnp.float32)
    cache = cache_ref[...]
    latent = latent_ref[...]
    step = 2
    causal = iota((step * TOK, TOK), 1) <= iota((step * TOK, TOK), 0) % TOK
    for h in range(0, HEADS, step):
        q = q_s[h * TOK : (h + step) * TOK, :]
        s_old = dot_nt(q, cache) + bias
        s_new = jnp.where(causal, dot_nt(q, latent), -1e30)
        largest = jnp.maximum(
            jnp.max(s_old, axis=1, keepdims=True), jnp.max(s_new, axis=1, keepdims=True)
        )
        e_old = jnp.exp((s_old - largest) * scale)
        e_new = jnp.exp((s_new - largest) * scale)
        total = jnp.sum(e_old, axis=1, keepdims=True) + jnp.sum(e_new, axis=1, keepdims=True)
        mixed = dot32(e_old.astype(jnp.bfloat16), cache[:, :LATENT])
        mixed = mixed + dot32(e_new.astype(jnp.bfloat16), latent[:, :LATENT])
        mixed = (mixed / total).astype(jnp.bfloat16)
        for i in range(step):
            cols = slice((h + i) * VHEAD, (h + i + 1) * VHEAD)
            values = dot32(mixed[i * TOK : (i + 1) * TOK], value_up_ref[:, cols])
            mid_s[:, cols] = (residual_ref[:, cols].astype(jnp.float32) + values).astype(jnp.bfloat16)
    middle = mid_s[...]
    middle_ref[...] = middle
    middle_f = middle.astype(jnp.float32)
    mean = jnp.mean(middle_f * middle_f, axis=1, keepdims=True)
    payload_ref[:, :D] = (middle_f * lax.rsqrt(mean + 1e-06) * gain_ref[...]).astype(jnp.bfloat16)
    lane = iota((TOK, EXTRA), 1)
    dense = jnp.zeros((TOK, EXTRA), jnp.float32)
    for k in range(TOP):
        dense = dense + jnp.where(routes_ref[:, k : k + 1] == lane % EXPERTS, gates_ref[:, k : k + 1], 0.0)
    high = dense.astype(jnp.bfloat16).astype(jnp.float32)
    cols = jnp.where(lane < EXPERTS, high, jnp.where(lane < 2 * EXPERTS, dense - high, 0.0))
    payload_ref[:, D:] = cols.astype(jnp.bfloat16)


def attend(length, queries, latent, cache, residual, value_up, gain, routes, gates):
    return pl.pallas_call(
        attend_kernel,
        out_shape=(
            jax.ShapeDtypeStruct((TOK, D + EXTRA), jnp.bfloat16),
            jax.ShapeDtypeStruct((TOK, D), jnp.bfloat16),
        ),
        in_specs=[SMEM] + [VMEM] * 8,
        out_specs=(VMEM, VMEM),
        scratch_shapes=[
            pltpu.VMEM((HEADS * TOK, KEY), jnp.bfloat16),
            pltpu.VMEM((TOK, D), jnp.bfloat16),
        ],
        compiler_params=pltpu.CompilerParams(vmem_limit_bytes=32 * 1024 * 1024),
        cost_estimate=pl.CostEstimate(flops=900_000_000, bytes_accessed=2_500_000, transcendentals=700_000),
        name="attend",
    )(length, queries, latent, cache, residual, value_up, gain.reshape(1, D), routes, gates)


def expert_of(member, near):
    return (member // 2) * 8 + (near + member % 2) % 8


def select_kernel(near_ref, hub_ref, out_ref):
    near = near_ref[0]
    rows = RANKS * TOK
    hub = hub_ref[...].reshape(rows, D + EXTRA)
    lane = iota((MEMBERS, EXTRA), 1)
    pick = lane == expert_of(iota((MEMBERS, EXTRA), 0), near)
    chosen = dot_nt(pick.astype(jnp.bfloat16), hub[:, D:])
    taken = chosen > 0.0
    first, second = iota((rows, rows), 0), iota((rows, rows), 1)
    upto = (first // TOK == second // TOK) & (first <= second)
    counts = dot32(taken.astype(jnp.bfloat16), upto.astype(jnp.bfloat16)).astype(jnp.int32)
    slot = counts - 1 + CAP * (iota((MEMBERS, rows), 1) // TOK)
    slot = jnp.where(taken, slot, -1)
    sel = slot[:, None, :] == iota((MEMBERS, SLOTS, rows), 1)
    sel = sel.astype(jnp.float32).reshape(MEMBERS * SLOTS, rows).astype(jnp.bfloat16)
    out_ref[...] = dot32(sel, hub[:, :D]).astype(jnp.bfloat16)


def select(near, hub):
    return pl.pallas_call(
        select_kernel,
        out_shape=jax.ShapeDtypeStruct((MEMBERS * SLOTS, D), jnp.bfloat16),
        in_specs=[SMEM, VMEM],
        out_specs=VMEM,
        compiler_params=pltpu.CompilerParams(vmem_limit_bytes=32 * 1024 * 1024),
        cost_estimate=pl.CostEstimate(flops=400_000_000, bytes_accessed=2_300_000, transcendentals=0),
        name="select",
    )(near, hub)


def combine_kernel(near_ref, cols_ref, back_ref, out_ref):
    near = near_ref[0]
    rows = RANKS * TOK
    wide = MEMBERS * SLOTS
    cols = cols_ref[...].reshape(rows, EXTRA)
    lane = iota((EXTRA, wide), 0)
    expert = expert_of(iota((EXTRA, wide), 1) // SLOTS, near)
    high = dot32(cols, (lane == expert).astype(jnp.bfloat16))
    low = dot32(cols, (lane == expert + EXPERTS).astype(jnp.bfloat16))
    taken = (high > 0.0).astype(jnp.bfloat16)
    first, second = iota((rows, rows), 0), iota((rows, rows), 1)
    upto = (first // TOK == second // TOK) & (second <= first)
    counts = dot32(upto.astype(jnp.bfloat16), taken).astype(jnp.int32)
    slot = counts - 1 + CAP * (iota((rows, wide), 0) // TOK)
    here = (slot == iota((rows, wide), 1) % SLOTS) & (high > 0.0)
    back = back_ref[...]
    mixed = dot32(jnp.where(here, high, 0.0).astype(jnp.bfloat16), back)
    mixed = mixed + dot32(jnp.where(here, low, 0.0).astype(jnp.bfloat16), back)
    out_ref[...] = mixed.astype(jnp.bfloat16)


def combine(near, cols, back):
    return pl.pallas_call(
        combine_kernel,
        out_shape=jax.ShapeDtypeStruct((RANKS * TOK, D), jnp.bfloat16),
        in_specs=[SMEM, VMEM, VMEM],
        out_specs=VMEM,
        compiler_params=pltpu.CompilerParams(vmem_limit_bytes=32 * 1024 * 1024),
        cost_estimate=pl.CostEstimate(flops=800_000_000, bytes_accessed=2_300_000, transcendentals=0),
        name="combine",
    )(near, cols, back)


def expert_kernel(x_ref, gate_ref, up_ref, down_ref, other_ref, out_ref, wg, wu, wd, hidden, sem):
    copies = []

    def fetch(src, dst):
        copies.append(pltpu.make_async_copy(src, dst, sem.at[len(copies)]))

    at = 0
    for mine, w in ((gate_ref, wg), (up_ref, wu)):
        fetch(mine, w.at[:, :, pl.ds(0, FF)])
        for c in range(GBLOCKS):
            fetch(other_ref.at[:, pl.ds(at, GROWS), :], w.at[:, :, pl.ds(FF + c * 128, 128)])
            at += GROWS
    first = len(copies)
    fetch(down_ref, wd.at[0])
    for c in range(DBLOCKS):
        fetch(other_ref.at[:, pl.ds(at, DROWS), :], wd.at[1, :, :, pl.ds(c * 128, 128)])
        at += DROWS
    for copy in copies:
        copy.start()
    for copy in copies[:first]:
        copy.wait()
    x = x_ref[...]
    for n in range(0, 2 * FF, 256):
        gate = dot32(x, wg[:, :, n : n + 256].reshape(D, 256))
        upper = dot32(x, wu[:, :, n : n + 256].reshape(D, 256))
        hidden[:, n : n + 256] = (gate / (1.0 + jnp.exp(-gate)) * upper).astype(jnp.bfloat16)
    for copy in copies[first:]:
        copy.wait()
    for n in range(0, D, 256):
        out_ref[:, n : n + 256] = dot32(
            hidden[...], wd[:, :, :, n : n + 256].reshape(2 * FF, 256)
        ).astype(jnp.bfloat16)


def expert(x, gate, up, down, other):
    rows = x.shape[0]
    return pl.pallas_call(
        expert_kernel,
        out_shape=jax.ShapeDtypeStruct((rows, D), jnp.bfloat16),
        in_specs=[VMEM, ANY, ANY, ANY, ANY],
        out_specs=VMEM,
        scratch_shapes=[
            pltpu.VMEM((GROUP, GROWS, 2 * FF), jnp.bfloat16),
            pltpu.VMEM((GROUP, GROWS, 2 * FF), jnp.bfloat16),
            pltpu.VMEM((2, GROUP, DROWS, D), jnp.bfloat16),
            pltpu.VMEM((rows, 2 * FF), jnp.bfloat16),
            pltpu.SemaphoreType.DMA((2 * GBLOCKS + DBLOCKS + 3,)),
        ],
        compiler_params=pltpu.CompilerParams(vmem_limit_bytes=40 * 1024 * 1024),
        cost_estimate=pl.CostEstimate(
            flops=6 * rows * D * 2 * FF, bytes_accessed=9_000_000, transcendentals=rows * 2 * FF
        ),
        name="expert",
    )(
        x,
        gate.reshape(GROUP, GROWS, FF),
        up.reshape(GROUP, GROWS, FF),
        down.reshape(GROUP, DROWS, D),
        other,
    )


def exchange(x, groups):
    return lax.all_to_all(
        x, "dp", split_axis=0, concat_axis=0, axis_index_groups=groups, tiled=True
    )


def on_device(
    queries,
    latent,
    cache,
    residual,
    value_up,
    norm_gain,
    cache_lengths,
    routes,
    route_gates,
    expert_gate,
    expert_up,
    expert_down,
):
    weights = expert_gate[0], expert_up[0], expert_down[0]
    mine = lax.axis_index("group").astype(jnp.int32).reshape(1)
    eighth = lax.ppermute(pack(mine, *weights), "dp", SWAP)
    other = lax.all_gather(eighth, "group", axis=0, tiled=False)

    payload, middle = attend(
        cache_lengths, queries, latent, cache, residual, value_up, norm_gain, routes, route_gates
    )
    position = lax.axis_index("dp") % NZ
    near = (((position + NZ - 1) % NZ) // 2).astype(jnp.int32).reshape(1)
    hub = exchange(jnp.broadcast_to(payload[None], (RANKS,) + payload.shape), FAR)
    outgoing = select(near, hub).reshape(MEMBERS, SLOTS, D)
    arrived = exchange(outgoing, NEAR).reshape(MEMBERS * SLOTS, D)
    finished = expert(arrived, *weights, other).reshape(MEMBERS, SLOTS, D)
    returned = exchange(finished, NEAR).reshape(MEMBERS * SLOTS, D)
    mixed = combine(near, hub[:, :, D:], returned).reshape(RANKS, TOK, D)
    mixture = jnp.sum(exchange(mixed, FAR).astype(jnp.float32), axis=0)
    return (middle.astype(jnp.float32) + mixture).astype(jnp.bfloat16)


def solution(mesh):
    return jax.shard_map(
        on_device,
        mesh=mesh,
        in_specs=(
            P(("group", "dp"), None),
            P(("group", "dp"), None),
            P(("group", "dp"), None),
            P(("group", "dp"), None),
            P(),
            P(),
            P(("group", "dp")),
            P(("group", "dp"), None),
            P(("group", "dp"), None),
            P("dp", None, None),
            P("dp", None, None),
            P("dp", None, None),
        ),
        out_specs=P(("group", "dp"), None),
        check_vma=False,
    )
```

```python
import jax
import jax.numpy as jnp
from jax import lax
from jax.experimental import pallas as pl
from jax.experimental.pallas import tpu as pltpu
from jax.sharding import PartitionSpec as P

HEADS = 10
VHEAD = 128
LATENT = 256
ROPE = 64
KEY = LATENT + ROPE
TOP = 6
NY = 4
NZ = 16
CAP = 18
EXPERTS = 32
EXTRA = 128
GROUP = 8
RANKS = 4
MEMBERS = 8
SLOTS = RANKS * CAP
TOK = 64
D = 1280
FF = 384

FAR = [[y * NZ + 4 * q + r for q in range(4)] for y in range(NY) for r in range(4)]
NEAR = [
    [y * NZ + (2 * k + 1 + s) % NZ for y in range(NY) for s in range(2)] for k in range(NZ // 2)
]
SWAP = [(i, i ^ 1) for i in range(NY * NZ)]

VMEM = pl.BlockSpec(memory_space=pltpu.VMEM)
SMEM = pl.BlockSpec(memory_space=pltpu.SMEM)
HBM = pl.BlockSpec(memory_space=pltpu.HBM)


def dot32(a, b):
    return jnp.dot(a, b, preferred_element_type=jnp.float32)


def dot_nt(a, b):
    return lax.dot_general(a, b, (((1,), (1,)), ((), ())), preferred_element_type=jnp.float32)


def iota(shape, dim):
    return lax.broadcasted_iota(jnp.int32, shape, dim)


GROWS = D // GROUP
DROWS = FF // GROUP
GBLOCKS = FF // 128
DBLOCKS = D // 128
PACKED = 2 * GBLOCKS * GROWS + DBLOCKS * DROWS


def pack_kernel(mine_ref, gate_ref, up_ref, down_ref, out_ref):
    at = 0
    for ref, rows, blocks in (
        (gate_ref, GROWS, GBLOCKS),
        (up_ref, GROWS, GBLOCKS),
        (down_ref, DROWS, DBLOCKS),
    ):
        for c in range(blocks):
            out_ref[at : at + rows, :] = ref[0, :, c * 128 : (c + 1) * 128]
            at += rows


def pack(mine, gate, up, down):
    def slice_of(i, mine_ref):
        return mine_ref[0], 0, 0

    return pl.pallas_call(
        pack_kernel,
        out_shape=jax.ShapeDtypeStruct((PACKED, 128), jnp.bfloat16),
        grid_spec=pltpu.PrefetchScalarGridSpec(
            num_scalar_prefetch=1,
            grid=(1,),
            in_specs=[
                pl.BlockSpec((1, GROWS, FF), slice_of),
                pl.BlockSpec((1, GROWS, FF), slice_of),
                pl.BlockSpec((1, DROWS, D), slice_of),
            ],
            out_specs=pl.BlockSpec((PACKED, 128), lambda i, mine_ref: (0, 0)),
        ),
        cost_estimate=pl.CostEstimate(flops=0, bytes_accessed=4 * PACKED * 128, transcendentals=0),
        name="pack",
    )(mine, gate.reshape(GROUP, GROWS, FF), up.reshape(GROUP, GROWS, FF), down.reshape(GROUP, DROWS, D))


def attend_kernel(
    length_ref, q_ref, latent_ref, cache_t_ref, residual_ref, value_up_ref, gain_ref, routes_t_ref, gates_t_ref,
    payload_ref, middle_ref, q_s, mid_s,
):
    scale = (VHEAD + ROPE) ** (-0.5)
    for h in range(HEADS):
        q_s[h * TOK : (h + 1) * TOK, :] = q_ref[:, h * KEY : (h + 1) * KEY]
    length = length_ref[0]
    prefix = cache_t_ref.shape[1]
    bias = jnp.where(iota((1, prefix), 1) < length, 0.0, -1e30).astype(jnp.float32)
    cache_t = cache_t_ref[...]
    latent = latent_ref[...]
    step = 2
    causal = iota((step * TOK, TOK), 1) <= iota((step * TOK, TOK), 0) % TOK
    for h in range(0, HEADS, step):
        q = q_s[h * TOK : (h + step) * TOK, :]
        s_old = dot32(q, cache_t) + bias
        s_new = jnp.where(causal, dot_nt(q, latent), -1e30)
        largest = jnp.maximum(
            jnp.max(s_old, axis=1, keepdims=True), jnp.max(s_new, axis=1, keepdims=True)
        )
        e_old = jnp.exp((s_old - largest) * scale)
        e_new = jnp.exp((s_new - largest) * scale)
        total = jnp.sum(e_old, axis=1, keepdims=True) + jnp.sum(e_new, axis=1, keepdims=True)
        mixed = dot_nt(e_old.astype(jnp.bfloat16), cache_t[:LATENT, :])
        mixed = mixed + dot32(e_new.astype(jnp.bfloat16), latent[:, :LATENT])
        mixed = (mixed / total).astype(jnp.bfloat16)
        for i in range(step):
            cols = slice((h + i) * VHEAD, (h + i + 1) * VHEAD)
            values = dot32(mixed[i * TOK : (i + 1) * TOK], value_up_ref[:, cols])
            mid_s[:, cols] = (residual_ref[:, cols].astype(jnp.float32) + values).astype(jnp.bfloat16)
    middle = mid_s[...]
    middle_ref[...] = middle
    middle_f = middle.astype(jnp.float32)
    mean = jnp.mean(middle_f * middle_f, axis=1, keepdims=True)
    payload_ref[:, :D] = (middle_f * lax.rsqrt(mean + 1e-06) * gain_ref[...].reshape(1, D)).astype(jnp.bfloat16)
    row = iota((EXTRA, TOK), 0)
    dense = jnp.zeros((EXTRA, TOK), jnp.float32)
    for k in range(TOP):
        dense = dense + jnp.where(routes_t_ref[k : k + 1, :] == row % EXPERTS, gates_t_ref[k : k + 1, :], 0.0)
    high = dense.astype(jnp.bfloat16).astype(jnp.float32)
    rows = jnp.where(row < EXPERTS, high, jnp.where(row < 2 * EXPERTS, dense - high, 0.0))
    same = (iota((TOK, TOK), 0) == iota((TOK, TOK), 1)).astype(jnp.bfloat16)
    payload_ref[:, D:] = dot_nt(same, rows.astype(jnp.bfloat16)).astype(jnp.bfloat16)


def attend(length, queries, latent, cache, residual, value_up, gain, routes, gates):
    return pl.pallas_call(
        attend_kernel,
        out_shape=(
            jax.ShapeDtypeStruct((TOK, D + EXTRA), jnp.bfloat16),
            jax.ShapeDtypeStruct((TOK, D), jnp.bfloat16),
        ),
        in_specs=[SMEM] + [VMEM] * 8,
        out_specs=(VMEM, VMEM),
        scratch_shapes=[
            pltpu.VMEM((HEADS * TOK, KEY), jnp.bfloat16),
            pltpu.VMEM((TOK, D), jnp.bfloat16),
        ],
        compiler_params=pltpu.CompilerParams(vmem_limit_bytes=32 * 1024 * 1024),
        cost_estimate=pl.CostEstimate(flops=900_000_000, bytes_accessed=2_500_000, transcendentals=700_000),
        name="attend",
    )(length, queries, latent, cache.T, residual, value_up, gain, routes.T, gates.T)


def expert_of(member, near):
    return (member // 2) * 8 + (near + member % 2) % 8


def select_kernel(near_ref, hub_ref, out_ref):
    near = near_ref[0]
    rows = RANKS * TOK
    hub = hub_ref[...].reshape(rows, D + EXTRA)
    lane = iota((MEMBERS, EXTRA), 1)
    pick = lane == expert_of(iota((MEMBERS, EXTRA), 0), near)
    chosen = dot_nt(pick.astype(jnp.bfloat16), hub[:, D:])
    taken = chosen > 0.0
    first, second = iota((rows, rows), 0), iota((rows, rows), 1)
    upto = (first // TOK == second // TOK) & (first <= second)
    counts = dot32(taken.astype(jnp.bfloat16), upto.astype(jnp.bfloat16)).astype(jnp.int32)
    slot = counts - 1 + CAP * (iota((MEMBERS, rows), 1) // TOK)
    slot = jnp.where(taken, slot, -1)
    sel = slot[:, None, :] == iota((MEMBERS, SLOTS, rows), 1)
    sel = sel.astype(jnp.float32).reshape(MEMBERS * SLOTS, rows).astype(jnp.bfloat16)
    out_ref[...] = dot32(sel, hub[:, :D]).astype(jnp.bfloat16)


def select(near, hub):
    return pl.pallas_call(
        select_kernel,
        out_shape=jax.ShapeDtypeStruct((MEMBERS * SLOTS, D), jnp.bfloat16),
        in_specs=[SMEM, VMEM],
        out_specs=VMEM,
        compiler_params=pltpu.CompilerParams(vmem_limit_bytes=32 * 1024 * 1024),
        cost_estimate=pl.CostEstimate(flops=400_000_000, bytes_accessed=2_300_000, transcendentals=0),
        name="select",
    )(near, hub)


def combine_kernel(near_ref, cols_ref, back_ref, out_ref):
    near = near_ref[0]
    rows = RANKS * TOK
    wide = MEMBERS * SLOTS
    cols = cols_ref[...].reshape(rows, EXTRA)
    lane = iota((EXTRA, wide), 0)
    expert = expert_of(iota((EXTRA, wide), 1) // SLOTS, near)
    high = dot32(cols, (lane == expert).astype(jnp.bfloat16))
    low = dot32(cols, (lane == expert + EXPERTS).astype(jnp.bfloat16))
    taken = (high > 0.0).astype(jnp.bfloat16)
    first, second = iota((rows, rows), 0), iota((rows, rows), 1)
    upto = (first // TOK == second // TOK) & (second <= first)
    counts = dot32(upto.astype(jnp.bfloat16), taken).astype(jnp.int32)
    slot = counts - 1 + CAP * (iota((rows, wide), 0) // TOK)
    here = (slot == iota((rows, wide), 1) % SLOTS) & (high > 0.0)
    back = back_ref[...]
    mixed = dot32(jnp.where(here, high, 0.0).astype(jnp.bfloat16), back)
    mixed = mixed + dot32(jnp.where(here, low, 0.0).astype(jnp.bfloat16), back)
    out_ref[...] = mixed.astype(jnp.bfloat16)


def combine(near, cols, back):
    return pl.pallas_call(
        combine_kernel,
        out_shape=jax.ShapeDtypeStruct((RANKS * TOK, D), jnp.bfloat16),
        in_specs=[SMEM, VMEM, VMEM],
        out_specs=VMEM,
        compiler_params=pltpu.CompilerParams(vmem_limit_bytes=32 * 1024 * 1024),
        cost_estimate=pl.CostEstimate(flops=800_000_000, bytes_accessed=2_300_000, transcendentals=0),
        name="combine",
    )(near, cols, back)


def expert_kernel(x_ref, gate_ref, up_ref, down_ref, other_ref, out_ref, wg, wu, wd, hidden, done, sem):
    copies = []

    def fetch(src, dst):
        copies.append(pltpu.make_async_copy(src, dst, sem.at[len(copies)]))

    at = 0
    for mine, w in ((gate_ref, wg), (up_ref, wu)):
        fetch(mine, w.at[:, :, pl.ds(0, FF)])
        for c in range(GBLOCKS):
            fetch(other_ref.at[:, pl.ds(at, GROWS), :], w.at[:, :, pl.ds(FF + c * 128, 128)])
            at += GROWS
    first = len(copies)
    fetch(down_ref, wd.at[0])
    for c in range(DBLOCKS):
        fetch(other_ref.at[:, pl.ds(at, DROWS), :], wd.at[1, :, :, pl.ds(c * 128, 128)])
        at += DROWS
    for copy in copies:
        copy.start()
    for copy in copies[:first]:
        copy.wait()
    x = x_ref[...]
    for n in range(0, 2 * FF, 256):
        gate = dot32(x, wg[:, :, n : n + 256].reshape(D, 256))
        upper = dot32(x, wu[:, :, n : n + 256].reshape(D, 256))
        hidden[:, n : n + 256] = (gate / (1.0 + jnp.exp(-gate)) * upper).astype(jnp.bfloat16)
    for copy in copies[first:]:
        copy.wait()
    sends = []
    for i, n in enumerate(range(0, D, 256)):
        done[i] = dot32(hidden[...], wd[:, :, :, n : n + 256].reshape(2 * FF, 256)).astype(jnp.bfloat16)
        sends.append(
            pltpu.make_async_copy(
                done.at[i], out_ref.at[:, pl.ds(n, 256)], sem.at[len(copies) + i]
            )
        )
        sends[-1].start()
    for send in sends:
        send.wait()


def expert(x, gate, up, down, other):
    rows = x.shape[0]
    return pl.pallas_call(
        expert_kernel,
        out_shape=jax.ShapeDtypeStruct((rows, D), jnp.bfloat16),
        in_specs=[VMEM, HBM, HBM, HBM, HBM],
        out_specs=HBM,
        scratch_shapes=[
            pltpu.VMEM((GROUP, GROWS, 2 * FF), jnp.bfloat16),
            pltpu.VMEM((GROUP, GROWS, 2 * FF), jnp.bfloat16),
            pltpu.VMEM((2, GROUP, DROWS, D), jnp.bfloat16),
            pltpu.VMEM((rows, 2 * FF), jnp.bfloat16),
            pltpu.VMEM((D // 256, rows, 256), jnp.bfloat16),
            pltpu.SemaphoreType.DMA((2 * GBLOCKS + DBLOCKS + 3 + D // 256,)),
        ],
        compiler_params=pltpu.CompilerParams(vmem_limit_bytes=60 * 1024 * 1024),
        cost_estimate=pl.CostEstimate(
            flops=6 * rows * D * 2 * FF, bytes_accessed=9_000_000, transcendentals=rows * 2 * FF
        ),
        name="expert",
    )(
        x,
        gate.reshape(GROUP, GROWS, FF),
        up.reshape(GROUP, GROWS, FF),
        down.reshape(GROUP, DROWS, D),
        other,
    )


def exchange(x, groups):
    return lax.all_to_all(
        x, "dp", split_axis=0, concat_axis=0, axis_index_groups=groups, tiled=True
    )


def on_device(
    queries,
    latent,
    cache,
    residual,
    value_up,
    norm_gain,
    cache_lengths,
    routes,
    route_gates,
    expert_gate,
    expert_up,
    expert_down,
):
    weights = expert_gate[0], expert_up[0], expert_down[0]
    mine = lax.axis_index("group").astype(jnp.int32).reshape(1)
    packed, queries = lax.optimization_barrier((pack(mine, *weights), queries))
    eighth = lax.ppermute(packed, "dp", SWAP)
    payload, middle = attend(
        cache_lengths, queries, latent, cache, residual, value_up, norm_gain, routes, route_gates
    )
    eighth, payload = lax.optimization_barrier((eighth, payload))
    other = lax.all_gather(eighth, "group", axis=0, tiled=False)
    position = lax.axis_index("dp") % NZ
    near = (((position + NZ - 1) % NZ) // 2).astype(jnp.int32).reshape(1)
    hub = lax.all_gather(payload, "dp", axis=0, axis_index_groups=FAR, tiled=False)
    outgoing = select(near, hub).reshape(MEMBERS, SLOTS, D)
    outgoing, other = lax.optimization_barrier((outgoing, other))
    arrived = exchange(outgoing, NEAR).reshape(MEMBERS * SLOTS, D)
    finished = expert(arrived, *weights, other).reshape(MEMBERS, SLOTS, D)
    returned = exchange(finished, NEAR).reshape(MEMBERS * SLOTS, D)
    mixed = combine(near, hub[:, :, D:], returned).reshape(RANKS, TOK, D)
    mixture = jnp.sum(exchange(mixed, FAR).astype(jnp.float32), axis=0)
    return (middle.astype(jnp.float32) + mixture).astype(jnp.bfloat16)


def solution(mesh):
    return jax.shard_map(
        on_device,
        mesh=mesh,
        in_specs=(
            P(("group", "dp"), None),
            P(("group", "dp"), None),
            P(("group", "dp"), None),
            P(("group", "dp"), None),
            P(),
            P(),
            P(("group", "dp")),
            P(("group", "dp"), None),
            P(("group", "dp"), None),
            P("dp", None, None),
            P("dp", None, None),
            P("dp", None, None),
        ),
        out_specs=P(("group", "dp"), None),
        check_vma=False,
    )
```
